256 devices in a mesh: leaf: 16 (over z, core), probe: 16 (over y, x).
Axes of the slice: x: 4, y: 4, z: 8, core: 2. Of those that a mesh axis runs over, the one named last changes fastest.
Arguments:
- points: bfloat16 [8, 65536], P(None, 'leaf'), may hold values from -6 to 6
- values: bfloat16 [64, 65536], P('probe', 'leaf'), may hold values from -6 to 6
- order: int32 [16, 4096], P('leaf'), may hold values from 0 to 4095, each once within a row
- block_list: int32 [256, 8], P('leaf'), may hold values from 0 to 255, as said below
- leaf_basis: bfloat16 [256, 256, 256], P('leaf'), may hold values from -0.375 to 0.375
- local_transfers: bfloat16 [16, 30, 2, 256, 256], P('leaf'), may hold values from -0.25 to 0.25
- chain_transfers: bfloat16 [16, 4, 2, 256, 256], P('leaf', None, None, 'probe'), as said below
Outputs:
- product: float32 [64, 65536], P('probe', 'leaf')
The draws below stay inside these ranges and needn't reach their ends.
Inputs may be any that keep to these rules, and one draw needn't show every extreme that they name: `block_list`: row i lists leaf i first, then 8 - 1 leaves j with 1 <= |j - i| <= 16; entries may repeat. `order`: each row is a permutation. `chain_transfers`: slot j of device d holds the pair of the level 4 + j node above d; all devices under one node hold the same pair.
All inputs are finite; a program needn't handle non-finite values.
Results may differ from the reference program's by a relative error of at most 0.0028.
Values may be sent and summed in bfloat16 or wider, within the bound.
No kernel may reach another device: no remote copies, remote signals or barrier semaphores. Data moves between devices by JAX's collectives and lax.ppermute only.
A program may use at most 64 MiB of HBM per device.

```python
import jax
import jax.numpy as jnp
import numpy as np
from jax import lax

DIM = 8
LEAF = 256
RANK = 256
PROBES = 64
NEAR = 8
LOCAL = 4
LEAF_DEV = 16
CHAIN = 4
LEAVES = 256
PTS_DEV = 4096
POINTS = 65536
LOCAL_NODES = 30
N_LEAF = 16


def draw_block_list(key, part):
    nonzero = jnp.concatenate([-jnp.arange(1, LEAF_DEV + 1, dtype=jnp.int32), jnp.arange(1, LEAF_DEV + 1, dtype=jnp.int32)])
    row_keys = jax.random.split(key, LEAVES)
    offsets = jax.vmap(lambda subkey: jax.random.permutation(subkey, nonzero)[:NEAR - 1])(row_keys)
    offsets = offsets.at[0, 0].set(LEAF_DEV)
    itself = jnp.arange(LEAVES, dtype=jnp.int32)[:, None]
    forward = itself + offsets
    inside = jnp.logical_and(forward >= 0, forward < LEAVES)
    picked = jnp.where(inside, forward, itself - offsets)
    return jnp.concatenate([itself, picked], 1).astype(jnp.int32)


def draw_chain_transfers(key, part):
    devices = np.arange(N_LEAF)
    owners = np.stack([devices >> level_shift << level_shift for level_shift in range(CHAIN)], 1)
    node_table = owners * CHAIN + np.arange(CHAIN)[None, :]

    def one_device(node_ids):

        def one_node(node_index):
            node_key = jax.random.fold_in(key, node_index)
            sample = jax.random.normal(node_key, (2, RANK, RANK), jnp.float32)
            return (sample * (2.0 * RANK) ** (-0.5)).astype(jnp.bfloat16)
        return jax.vmap(one_node)(node_ids)
    return lax.map(one_device, jnp.asarray(node_table, dtype=jnp.int32))


def level_of(rng, dims, pieces, least, largest):
    def one(dim, shards_of):
        draws = jax.random.uniform(jax.random.fold_in(jax.random.fold_in(rng, 6), dim), (shards_of,), jnp.float32, least / len(pieces), largest / len(pieces))
        return jnp.repeat(jnp.exp(draws), dims[dim] // shards_of).reshape((-1,) + (1,) * (len(dims) - dim - 1))

    factor_of = one(*pieces[0])
    for cut in pieces[1:]:
        factor_of = factor_of * one(*cut)
    return factor_of


def normal_values(stream_key, dims, width, bound, cuts=(), kind=jnp.bfloat16):
    loudness = level_of(stream_key, dims, cuts, -0.22, 0.18) if cuts else 1.0
    entries = jax.random.normal(stream_key, dims, jnp.float32) * width * loudness
    return jnp.minimum(jnp.maximum(entries, -bound), bound).astype(kind)


def setup_inputs(seed: int = 0) -> dict:
    key_list = jax.random.split(jax.random.key(seed), 8)
    return {
        "points": normal_values(key_list[0], (DIM, POINTS), 1.0, 6.0, ((1, 16),)),
        "values": normal_values(key_list[1], (PROBES, POINTS), 1.0, 6.0, ((0, 16), (1, 16))),
        "order": jax.vmap(lambda own: jax.random.permutation(own, PTS_DEV))(jax.random.split(key_list[2], N_LEAF)).reshape((N_LEAF, PTS_DEV)).astype(jnp.int32),
        "block_list": draw_block_list(jax.random.fold_in(key_list[7], 71), 0),
        "leaf_basis": normal_values(key_list[4], (LEAVES, LEAF, RANK), LEAF ** -0.5, 0.375, ((0, 16),)),
        "local_transfers": normal_values(key_list[5], (N_LEAF, LOCAL_NODES, 2, RANK, RANK), (2 * RANK) ** -0.5, 0.25, ((0, 16),)),
        "chain_transfers": draw_chain_transfers(jax.random.fold_in(key_list[7], 71), 0),
    }


PRECISE = lax.Precision.HIGHEST


def kernel_tile(source, target):
    source = source.astype(jnp.float32)
    target = target.astype(jnp.float32)
    inner_prod = jnp.einsum("dnq,dp->nqp", source, target, precision=PRECISE)
    squared = jnp.sum(source * source, 0)[:, :, None] + jnp.sum(target * target, 0)[None, None, :] - 2.0 * inner_prod
    factor = 1.0 + squared * 0.125
    return 1.0 / (factor * factor * factor)


def pair_fields(partial_value):
    upward = partial_value[:, 0]
    coupled = partial_value[:, 1]
    node_count = upward.shape[0]
    merged = upward[0::2] + upward[1::2]
    crossed = coupled.reshape(node_count // 2, 2, coupled.shape[1], coupled.shape[2])[:, ::-1].reshape(coupled.shape)
    return merged, crossed


def lift_terms(matrices, skeleton):
    return jnp.einsum("nmab,nac->nmbc", matrices.astype(jnp.float32), skeleton, precision=PRECISE)


def push_down(matrices, parent):
    return jnp.einsum("nab,nbc->nac", matrices.astype(jnp.float32), parent, precision=PRECISE)


def reference(points, values, order, block_list, leaf_basis, local_transfers, chain_transfers):
    positions = (order + (jnp.arange(N_LEAF, dtype=jnp.int32) * PTS_DEV)[:, None]).reshape(-1).astype(jnp.int32)
    coords = jnp.take(points, positions, axis=1).reshape(DIM, LEAVES, LEAF)
    values_tree = jnp.take(values, positions, axis=1).reshape(PROBES, LEAVES, LEAF)

    def near_leaf(leaf_index):
        picked_coords = jnp.take(coords, block_list[leaf_index], axis=1)
        picked_values = jnp.take(values_tree, block_list[leaf_index], axis=1)
        own_coords = lax.dynamic_index_in_dim(coords, leaf_index, 1, keepdims=False)
        near_tile = kernel_tile(picked_coords, own_coords).astype(jnp.bfloat16)
        return jnp.einsum("cnq,nqp->cp", picked_values.astype(jnp.float32), near_tile.astype(jnp.float32), precision=PRECISE)

    near_part = lax.map(near_leaf, jnp.arange(LEAVES, dtype=jnp.int32))
    skeleton = jnp.einsum("lqr,clq->lrc", leaf_basis.astype(jnp.float32), values_tree.astype(jnp.float32), precision=PRECISE)
    fields = []
    slot_start = 0
    for tree_level in range(LOCAL):
        node_count = LEAF_DEV >> tree_level
        matrices = local_transfers[:, slot_start:slot_start + node_count].reshape(N_LEAF * node_count, 2, RANK, RANK)
        skeleton, crossed = pair_fields(lift_terms(matrices, skeleton))
        fields.append(crossed)
        slot_start += node_count
    for chain_step in range(CHAIN):
        matrices = chain_transfers[::2 ** chain_step, chain_step]
        skeleton, crossed = pair_fields(lift_terms(matrices, skeleton))
        fields.append(crossed)
    node_field = jnp.zeros((1, RANK, PROBES), jnp.float32)
    for chain_step in range(CHAIN - 1, -1, -1):
        matrices = chain_transfers[::2 ** chain_step, chain_step, 0]
        node_field = fields[LOCAL + chain_step] + push_down(matrices, jnp.repeat(node_field, 2, axis=0))
    slot_start = 2 * LEAF_DEV - 2
    for tree_level in range(LOCAL - 1, -1, -1):
        node_count = LEAF_DEV >> tree_level
        slot_start -= node_count
        matrices = local_transfers[:, slot_start:slot_start + node_count, 0].reshape(N_LEAF * node_count, RANK, RANK)
        node_field = fields[tree_level] + push_down(matrices, jnp.repeat(node_field, 2, axis=0))
    far_part = jnp.einsum("lqr,lrc->clq", leaf_basis.astype(jnp.float32), node_field, precision=PRECISE)
    combined = jnp.transpose(near_part, (1, 0, 2)) + far_part
    flattened = combined.reshape(PROBES, POINTS)
    return jnp.zeros_like(flattened).at[:, positions].set(flattened)
```

```python
import functools
import jax
import jax.numpy as jnp
from jax import lax
from jax.experimental import pallas as pl
from jax.experimental.pallas import tpu as pltpu
from jax.sharding import PartitionSpec as P

F32 = jnp.float32
BF = jnp.bfloat16
MB = 2**20
NT = (((1,), (1,)), ((), ()))
NN = (((1,), (0,)), ((), ()))
VM = pl.BlockSpec(memory_space=pltpu.VMEM)
SM = pl.BlockSpec(memory_space=pltpu.SMEM)
ANY = pl.BlockSpec(memory_space=pl.ANY)


def dot(a, b, dims=NN):
    return lax.dot_general(a, b, dims, preferred_element_type=F32)


def split(s):
    hi = s.astype(BF).astype(F32)
    return jnp.concatenate([hi, s - hi], 0).astype(BF)


def dot2(left, mat, dims=NN):
    r = dot(left, mat, dims)
    return r[:8] + r[8:]


def tree_kernel(points, values, order, td, xs, xr):
    xs[0:8, :] = points[...].astype(F32)
    xs[8:16, :] = jnp.zeros((8, xs.shape[1]), F32)
    xs[8:12, :] = values[...].astype(F32)
    for h in range(16):
        xr[h * 16 : h * 16 + 16, :] = xs[:, h * 256 : h * 256 + 256].astype(BF)
    rows = lax.broadcasted_iota(jnp.int32, (256, 256), 0)
    sub = lax.broadcasted_iota(jnp.int32, (8, 256), 0)
    for t in range(16):
        o = order[:, t * 256 : t * 256 + 256]
        oh = jnp.where(rows == (o & 255), 1.0, 0.0).astype(BF)
        z = dot(xr[...], oh)
        hi = o >> 8
        low = jnp.zeros((8, 256), F32)
        high = jnp.zeros((8, 256), F32)
        for h in range(16):
            low = jnp.where(hi == h, z[h * 16 : h * 16 + 8], low)
            high = jnp.where(hi == h, z[h * 16 + 8 : h * 16 + 16], high)
        m = jnp.sum(low * low, 0, keepdims=True) * 0.125
        mh = m.astype(BF).astype(F32)
        high = jnp.where(sub == 4, mh, jnp.where(sub == 5, m - mh, jnp.where(sub >= 6, 1.0, high)))
        td[t] = jnp.concatenate([low, high], 0).astype(BF)


def tree(points, values, order):
    return pl.pallas_call(
        tree_kernel,
        out_shape=jax.ShapeDtypeStruct((16, 16, 256), BF),
        in_specs=[VM] * 3,
        out_specs=VM,
        scratch_shapes=[pltpu.VMEM((16, 4096), F32), pltpu.VMEM((256, 256), BF)],
        compiler_params=pltpu.CompilerParams(vmem_limit_bytes=8 * MB),
        name="tree",
    )(points, values, order)


LEVELS = ((0, 16), (16, 8), (24, 4), (28, 2))


def up_kernel(td, basis, lt, g, root, bas, ltv, s, sem):
    copies = []

    def start(src, dst):
        c = pltpu.make_async_copy(src, dst, sem.at[len(copies)])
        c.start()
        copies.append(c)

    for q in range(2):
        start(basis.at[pl.ds(q * 8, 8)], bas.at[pl.ds(q * 8, 8)])
    for q in range(4):
        start(lt.at[0, pl.ds(q * 4, 4)], ltv.at[pl.ds(q * 4, 4)])
    for q in range(2):
        start(lt.at[0, pl.ds(16 + q * 4, 4)], ltv.at[pl.ds(16 + q * 4, 4)])
    start(lt.at[0, pl.ds(24, 6)], ltv.at[pl.ds(24, 6)])
    sub = lax.broadcasted_iota(jnp.int32, (8, 256), 0)
    for l in range(16):
        if l % 8 == 0:
            copies[l // 8].wait()
        r = dot(td[l], bas[l])
        s[l] = jnp.where(sub < 4, r[8:], 0.0)
    for start_slot, count in LEVELS:
        for n in range(0, count, 2):
            slot = start_slot + n
            if slot % 4 == 0 and slot < 24:
                copies[2 + slot // 4].wait()
            if slot == 24:
                copies[8].wait()
            l0 = split(s[n])
            l1 = split(s[n + 1])
            g[slot + 1] = dot2(l0, ltv[slot, 1])
            g[slot] = dot2(l1, ltv[slot + 1, 1])
            s[n // 2] = dot2(l0, ltv[slot, 0]) + dot2(l1, ltv[slot + 1, 0])
    root[...] = s[0]


def up(td, basis, lt):
    return pl.pallas_call(
        up_kernel,
        out_shape=(jax.ShapeDtypeStruct((30, 8, 256), F32), jax.ShapeDtypeStruct((8, 256), F32)),
        in_specs=[VM, ANY, ANY],
        out_specs=(VM, VM),
        scratch_shapes=[
            pltpu.VMEM((16, 256, 256), BF),
            pltpu.VMEM((30, 2, 256, 256), BF),
            pltpu.VMEM((16, 8, 256), F32),
            pltpu.SemaphoreType.DMA((9,)),
        ],
        compiler_params=pltpu.CompilerParams(vmem_limit_bytes=16 * MB),
        name="up",
    )(td, basis, lt)


def near_kernel(variant, recip, unroll, slots, left, own, right, out, win, tr):
    win[0:16] = left[...]
    win[16:32] = own[...]
    win[32:48] = right[...]
    sub = lax.broadcasted_iota(jnp.int32, (16, 256), 0)

    def pside(l):
        p = own[l].astype(F32)
        m = jnp.sum(jnp.where(sub < 8, p * p, 0.0), 0, keepdims=True) * 0.125 + 1.0
        mh = m.astype(BF).astype(F32)
        return jnp.where(
            sub < 8, p * -0.25,
            jnp.where(sub < 12, 0.0, jnp.where(sub < 14, 1.0, jnp.where(sub == 14, mh, m - mh))))

    def inv(f):
        c = f * f * f
        if recip == "approx":
            return pl.reciprocal(c, approx=True).astype(BF)
        if recip == "newton":
            r = pl.reciprocal(c, approx=True)
            return (r * (2.0 - c * r)).astype(BF)
        return (1.0 / c).astype(BF)

    if variant == "A":
        def leaf(l, carry):
            pt = pside(l).T.astype(BF)
            acc = jnp.zeros((16, 256), F32)
            for n in range(8):
                q = win[slots[l, n]]
                f = dot(pt, q)
                acc = acc + dot(q, inv(f), NT)
            out[l] = acc[8:]
            return carry
    else:
        def tl(l, carry):
            tr[l] = win[l].astype(F32).T.astype(BF)
            return carry
        lax.fori_loop(0, 48, tl, 0, unroll=4)

        def leaf(l, carry):
            pt = pside(l).astype(BF)
            acc = jnp.zeros((16, 256), F32)
            for n in range(8):
                j = slots[l, n]
                f = dot(tr[j], pt)
                acc = acc + dot(win[j], inv(f))
            out[l] = acc[8:]
            return carry

    lax.fori_loop(0, 16, leaf, 0, unroll=unroll)


def near(slots, left, own, right, variant="A", recip="approx", unroll=1):
    return pl.pallas_call(
        functools.partial(near_kernel, variant, recip, unroll),
        out_shape=jax.ShapeDtypeStruct((16, 8, 256), F32),
        in_specs=[SM, VM, VM, VM],
        out_specs=VM,
        scratch_shapes=[pltpu.VMEM((48, 16, 256), BF), pltpu.VMEM((48, 256, 16), BF)],
        compiler_params=pltpu.CompilerParams(vmem_limit_bytes=16 * MB),
        name="near",
    )(slots, left, own, right)


def down_kernel(order, cf, near_f, g, chain, basis, lt, out, bas, ltv, f, cb, sem):
    copies = []

    def start(src, dst):
        c = pltpu.make_async_copy(src, dst, sem.at[len(copies)])
        c.start()
        copies.append(c)

    start(lt.at[0, pl.ds(24, 6), 0], ltv.at[pl.ds(24, 6)])
    start(lt.at[0, pl.ds(16, 8), 0], ltv.at[pl.ds(16, 8)])
    for q in range(2):
        start(lt.at[0, pl.ds(8 * q, 8), 0], ltv.at[pl.ds(8 * q, 8)])
    for q in range(2):
        start(basis.at[pl.ds(q * 8, 8)], bas.at[pl.ds(q * 8, 8)])
    top = cf[3]
    for k in (2, 1, 0):
        top = cf[k] + dot2(split(top), chain[2 * k], NT)
    f[0] = top
    for start_slot, count in LEVELS[::-1]:
        if start_slot == 28:
            copies[0].wait()
        if start_slot == 16:
            copies[1].wait()
        for m in range(count // 2 - 1, -1, -1):
            slot = start_slot + 2 * m
            if start_slot == 0 and m == 7:
                copies[3].wait()
            if start_slot == 0 and m == 3:
                copies[2].wait()
            l = split(f[m])
            f[2 * m + 1] = g[slot + 1] + dot2(l, ltv[slot + 1], NT)
            f[2 * m] = g[slot] + dot2(l, ltv[slot], NT)
    for l in range(16):
        if l % 8 == 0:
            copies[4 + l // 8].wait()
        tot = near_f[l] + dot2(split(f[l]), bas[l], NT)
        cb[:, l * 256 : l * 256 + 256] = tot
    rows = lax.broadcasted_iota(jnp.int32, (256, 256), 0)
    hrow = lax.broadcasted_iota(jnp.int32, (16, 256), 0)
    acc = jnp.zeros((128, 256), F32)
    for t in range(16):
        o = order[:, t * 256 : t * 256 + 256]
        oh = jnp.where(rows == (o & 255), 1.0, 0.0).astype(BF)
        hit = hrow == (o >> 8)
        c = cb[:, t * 256 : t * 256 + 256]
        ch = c.astype(BF).astype(F32)
        cl = c - ch
        parts = [jnp.where(hit, part[k : k + 1], 0.0) for k in range(4) for part in (ch, cl)]
        acc = acc + dot(jnp.concatenate(parts, 0).astype(BF), oh, NT)
    for k in range(4):
        both = acc[k * 32 : k * 32 + 16] + acc[k * 32 + 16 : k * 32 + 32]
        for h in range(16):
            out[k : k + 1, h * 256 : h * 256 + 256] = both[h : h + 1]


def down(order, cf, near_f, g, chain, basis, lt):
    return pl.pallas_call(
        down_kernel,
        out_shape=jax.ShapeDtypeStruct((4, 4096), F32),
        in_specs=[VM] * 5 + [ANY] * 2,
        out_specs=VM,
        scratch_shapes=[
            pltpu.VMEM((16, 256, 256), BF),
            pltpu.VMEM((30, 256, 256), BF),
            pltpu.VMEM((16, 8, 256), F32),
            pltpu.VMEM((8, 4096), F32),
            pltpu.SemaphoreType.DMA((6,)),
        ],
        compiler_params=pltpu.CompilerParams(vmem_limit_bytes=16 * MB),
        name="down",
    )(order, cf, near_f, g, chain, basis, lt)


def chain_kernel(*refs):
    root, groups, c, w, = refs[0], refs[1:5], refs[5], refs[6]
    me = lax.axis_index("probe")
    y, x = me // 4, lax.rem(me, 4)
    for ky in range(4):
        for kx in range(4):
            src = lax.rem(y + 4 - ky, 4) * 4 + lax.rem(x + 4 - kx, 4)
            at = pl.ds(pl.multiple_of(src * 16, 16), 16)
            for m in range(7):
                w[m, at, :] = groups[ky][kx, m]
    u = root[...]
    for k in range(4):
        left = split(u)
        c[k] = dot2(left, w[2 * k + 1 if k < 3 else 6])
        if k < 3:
            u = dot2(left, w[2 * k])


def chain(root, groups):
    return pl.pallas_call(
        chain_kernel,
        out_shape=(jax.ShapeDtypeStruct((4, 8, 256), F32), jax.ShapeDtypeStruct((7, 256, 256), BF)),
        in_specs=[VM] * 5,
        out_specs=(VM, VM),
        compiler_params=pltpu.CompilerParams(vmem_limit_bytes=8 * MB),
        name="chain",
    )(root, *groups)


def swapped(value, bit):
    return lax.ppermute(value, "leaf", [(i, i ^ (1 << bit)) for i in range(16)])


def shards(points, values, order, block_list, leaf_basis, local_transfers, chain_transfers):
    shard = chain_transfers[0].reshape(8, 16, 256)
    shard = jnp.concatenate([shard[:6], shard[7:]], 0)
    row = [shard] + [
        lax.ppermute(shard, "probe", [(i, i // 4 * 4 + (i + k) % 4) for i in range(16)])
        for k in range(1, 4)
    ]
    row = jnp.stack(row)
    groups = [row] + [
        lax.ppermute(row, "probe", [(i, (i + 4 * k) % 16) for i in range(16)]) for k in range(1, 4)
    ]
    own = tree(points, values, order)
    left = lax.ppermute(own, "leaf", [(i, (i + 1) % 16) for i in range(16)])
    right = lax.ppermute(own, "leaf", [(i, (i - 1) % 16) for i in range(16)])
    slots = block_list - (lax.axis_index("leaf") * 16 - 16)
    g, root = up(own, leaf_basis, local_transfers)
    near_f = near(slots, left, own, right)
    c, w = chain(root, groups)
    c = c[:, :4]
    cf = []
    for k in range(4):
        other = swapped(c, k)
        cf.append(other[0])
        c = c[1:] + other[1:]
    cf = jnp.stack(cf)
    cf = jnp.concatenate([cf, jnp.zeros_like(cf)], 1)
    return down(order, cf, near_f, g, w, leaf_basis, local_transfers)


def solution(mesh):
    placed = (
        P(None, "leaf"),
        P("probe", "leaf"),
        P("leaf", None),
        P("leaf", None),
        P("leaf", None, None),
        P("leaf", None, None, None, None),
        P("leaf", None, None, "probe", None),
    )
    return jax.shard_map(
        shards, mesh=mesh, in_specs=placed, out_specs=P("probe", "leaf"), check_vma=False
    )
```

```python
import functools
import jax
import jax.numpy as jnp
from jax import lax
from jax.experimental import pallas as pl
from jax.experimental.pallas import tpu as pltpu
from jax.sharding import PartitionSpec as P

F32 = jnp.float32
BF = jnp.bfloat16
MB = 2**20
NT = (((1,), (1,)), ((), ()))
NN = (((1,), (0,)), ((), ()))
VM = pl.BlockSpec(memory_space=pltpu.VMEM)
SM = pl.BlockSpec(memory_space=pltpu.SMEM)
HBM = pl.BlockSpec(memory_space=pltpu.HBM)


def dot(a, b, dims=NN):
    return lax.dot_general(a, b, dims, preferred_element_type=F32)


def split(s):
    hi = s.astype(BF).astype(F32)
    return jnp.concatenate([hi, s - hi], 0).astype(BF)


def dot2(left, mat, dims=NN):
    r = dot(left, mat, dims)
    return r[:8] + r[8:]


LEVELS = ((0, 16), (16, 8), (24, 4), (28, 2))


def starter(sem):
    copies = []

    def start(src, dst):
        copy = pltpu.make_async_copy(src, dst, sem.at[len(copies)])
        copy.start()
        copies.append(copy)

    return copies, start


def up_kernel(points, values, order, basis, lt, td, g, root, pv, vv, ov, xs, xr, bas, ltv, s, sem):
    copies, start = starter(sem)
    start(points, pv)
    start(values, vv)
    start(order, ov)
    for q in range(2):
        start(basis.at[pl.ds(q * 8, 8)], bas.at[pl.ds(q * 8, 8)])
    for q in range(4):
        start(lt.at[0, pl.ds(q * 4, 4)], ltv.at[pl.ds(q * 4, 4)])
    for q in range(2):
        start(lt.at[0, pl.ds(16 + q * 4, 4)], ltv.at[pl.ds(16 + q * 4, 4)])
    start(lt.at[0, pl.ds(24, 6)], ltv.at[pl.ds(24, 6)])
    for copy in copies[:3]:
        copy.wait()
    xs[0:8, :] = pv[...].astype(F32)
    xs[8:16, :] = jnp.zeros((8, xs.shape[1]), F32)
    xs[8:12, :] = vv[...].astype(F32)
    for h in range(16):
        xr[h * 16 : h * 16 + 16, :] = xs[:, h * 256 : h * 256 + 256].astype(BF)
    rows = lax.broadcasted_iota(jnp.int32, (256, 256), 0)
    sub = lax.broadcasted_iota(jnp.int32, (8, 256), 0)
    for t in range(16):
        o = ov[:, t * 256 : t * 256 + 256]
        oh = jnp.where(rows == (o & 255), 1.0, 0.0).astype(BF)
        z = dot(xr[...], oh)
        hi = o >> 8
        low = jnp.zeros((8, 256), F32)
        high = jnp.zeros((8, 256), F32)
        for h in range(16):
            low = jnp.where(hi == h, z[h * 16 : h * 16 + 8], low)
            high = jnp.where(hi == h, z[h * 16 + 8 : h * 16 + 16], high)
        m = jnp.sum(low * low, 0, keepdims=True) * 0.125
        mh = m.astype(BF).astype(F32)
        high = jnp.where(sub == 4, mh, jnp.where(sub == 5, m - mh, jnp.where(sub >= 6, 1.0, high)))
        td[t] = jnp.concatenate([low, high], 0).astype(BF)
    for l in range(16):
        if l % 8 == 0:
            copies[3 + l // 8].wait()
        r = dot(td[l], bas[l])
        s[l] = jnp.where(sub < 4, r[8:], 0.0)
    for start_slot, count in LEVELS:
        for n in range(0, count, 2):
            slot = start_slot + n
            if slot % 4 == 0 and slot < 24:
                copies[5 + slot // 4].wait()
            if slot == 24:
                copies[11].wait()
            l0 = split(s[n])
            l1 = split(s[n + 1])
            g[slot + 1] = dot2(l0, ltv[slot, 1])
            g[slot] = dot2(l1, ltv[slot + 1, 1])
            s[n // 2] = dot2(l0, ltv[slot, 0]) + dot2(l1, ltv[slot + 1, 0])
    root[...] = s[0]


def up(points, values, order, basis, lt):
    return pl.pallas_call(
        up_kernel,
        out_shape=(
            jax.ShapeDtypeStruct((16, 16, 256), BF),
            jax.ShapeDtypeStruct((30, 8, 256), F32),
            jax.ShapeDtypeStruct((8, 256), F32),
        ),
        in_specs=[HBM] * 5,
        out_specs=(VM, VM, VM),
        scratch_shapes=[
            pltpu.VMEM((8, 4096), BF),
            pltpu.VMEM((4, 4096), BF),
            pltpu.VMEM((1, 4096), jnp.int32),
            pltpu.VMEM((16, 4096), F32),
            pltpu.VMEM((256, 256), BF),
            pltpu.VMEM((16, 256, 256), BF),
            pltpu.VMEM((30, 2, 256, 256), BF),
            pltpu.VMEM((16, 8, 256), F32),
            pltpu.SemaphoreType.DMA((12,)),
        ],
        compiler_params=pltpu.CompilerParams(vmem_limit_bytes=16 * MB),
        name="up",
    )(points, values, order, basis, lt)


def sources(ref):
    p = ref[...].astype(F32)
    sub = lax.broadcasted_iota(jnp.int32, (16, 256), 0)
    m = jnp.sum(jnp.where(sub < 8, p * p, 0.0), 0, keepdims=True) * 0.125 + 1.0
    mh = m.astype(BF).astype(F32)
    p = jnp.where(
        sub < 8,
        p * -0.25,
        jnp.where(sub < 12, 0.0, jnp.where(sub < 14, 1.0, jnp.where(sub == 14, mh, m - mh))),
    )
    return p.T.astype(BF)


def block(pt, q):
    f = dot(pt, q)
    return dot(q, pltpu.reciprocal(f * f * f, approx=True).astype(BF), NT)[8:]


def near_own_kernel(own, out, pt):
    for l in range(16):
        pt[l] = sources(own.at[l])
        out[l] = block(pt[l], own[l])


def near_own(own):
    return pl.pallas_call(
        near_own_kernel,
        out_shape=(
            jax.ShapeDtypeStruct((16, 8, 256), F32),
            jax.ShapeDtypeStruct((16, 256, 16), BF),
        ),
        in_specs=[VM],
        out_specs=(VM, VM),
        compiler_params=pltpu.CompilerParams(vmem_limit_bytes=4 * MB),
        name="near_own",
    )(own)


def near_kernel(first, count, slot_ref, left, own, right, base, pt, out, win):
    slots = slot_ref[...]
    win[0:16] = left[...]
    win[16:32] = own[...]
    win[32:48] = right[...]
    for l in range(first, first + count):
        total = base[l]
        for n in range(1, 8):
            total = total + block(pt[l], win[slots[l, n]])
        out[l - first] = total


def near(first, count, slots, left, own, right, base, pt):
    return pl.pallas_call(
        functools.partial(near_kernel, first, count),
        out_shape=jax.ShapeDtypeStruct((count, 8, 256), F32),
        in_specs=[VM] * 6,
        out_specs=VM,
        scratch_shapes=[pltpu.VMEM((48, 16, 256), BF)],
        compiler_params=pltpu.CompilerParams(vmem_limit_bytes=8 * MB),
        name="near",
    )(slots, left, own, right, base, pt)


R1 = ((0, 0), (2, 0), (1, 2), (3, 2))
R2 = ((0, 0), (0, 1), (0, 3), (1, 0))


def shifted(value, shift):
    pairs = [
        (y * 4 + x, (y + shift[0]) % 4 * 4 + (x + shift[1]) % 4) for y in range(4) for x in range(4)
    ]
    return lax.ppermute(value, "probe", pairs)


def chain_kernel(*refs):
    root, groups, c, w = refs[0], refs[1:5], refs[5], refs[6]
    me = lax.axis_index("probe")
    y, x = me // 4, lax.rem(me, 4)
    for ky in range(4):
        for kx in range(4):
            sy = lax.rem(y + 8 - R2[ky][0] - R1[kx][0], 4)
            sx = lax.rem(x + 8 - R2[ky][1] - R1[kx][1], 4)
            at = pl.ds(pl.multiple_of((sy * 4 + sx) * 16, 16), 16)
            for m in range(7):
                w[m, at, :] = groups[ky][kx, m]
    u = root[...]
    for k in range(4):
        left = split(u)
        c[k] = dot2(left, w[2 * k + 1 if k < 3 else 6])
        if k < 3:
            u = dot2(left, w[2 * k])


def chain(root, groups):
    return pl.pallas_call(
        chain_kernel,
        out_shape=(jax.ShapeDtypeStruct((4, 8, 256), F32), jax.ShapeDtypeStruct((7, 256, 256), BF)),
        in_specs=[VM] * 5,
        out_specs=(VM, VM),
        compiler_params=pltpu.CompilerParams(vmem_limit_bytes=8 * MB),
        name="chain",
    )(root, *groups)


def down_kernel(
    order, o1, q1, q2, q3, o3, na, nb, nc, g, chain, basis, lt, out, ov, bas, ltv, f, ohs, sem
):
    copies, start = starter(sem)
    start(order, ov)
    start(lt.at[0, pl.ds(24, 6), 0], ltv.at[pl.ds(24, 6)])
    start(lt.at[0, pl.ds(16, 8), 0], ltv.at[pl.ds(16, 8)])
    for q in range(2):
        start(lt.at[0, pl.ds(8 * q, 8), 0], ltv.at[pl.ds(8 * q, 8)])
    for q in range(4):
        start(basis.at[pl.ds(q * 4, 4)], bas.at[pl.ds(q * 4, 4)])
    top = o3[0]
    for term, k in ((q2[0] + q3[0], 2), (q1[0], 1), (o1[0], 0)):
        top = term + dot2(split(top), chain[2 * k], NT)
    f[0] = top
    copies[0].wait()
    rows = lax.broadcasted_iota(jnp.int32, (256, 256), 0)
    for t in range(16):
        o = ov[:, t * 256 : t * 256 + 256]
        ohs[t] = jnp.where(rows == (o & 255), 1.0, 0.0).astype(BF)
    for start_slot, count in LEVELS[::-1]:
        if start_slot == 28:
            copies[1].wait()
        if start_slot == 16:
            copies[2].wait()
        if start_slot == 0:
            copies[3].wait()
            copies[4].wait()
        for m in range(count // 2 - 1, -1, -1):
            slot = start_slot + 2 * m
            l = split(f[m])
            f[2 * m + 1] = g[slot + 1] + dot2(l, ltv[slot + 1], NT)
            f[2 * m] = g[slot] + dot2(l, ltv[slot], NT)
    near_f = [r[i] for r in (na, nb, nc) for i in range(r.shape[0])]
    hrow = lax.broadcasted_iota(jnp.int32, (16, 256), 0)
    acc = jnp.zeros((128, 256), F32)
    for t in range(16):
        if t % 4 == 0:
            copies[5 + t // 4].wait()
        c = near_f[t] + dot2(split(f[t]), bas[t], NT)
        hit = hrow == (ov[:, t * 256 : t * 256 + 256] >> 8)
        ch = c.astype(BF).astype(F32)
        cl = c - ch
        parts = [jnp.where(hit, part[k : k + 1], 0.0) for k in range(4) for part in (ch, cl)]
        acc = acc + dot(jnp.concatenate(parts, 0).astype(BF), ohs[t], NT)
    for k in range(4):
        both = acc[k * 32 : k * 32 + 16] + acc[k * 32 + 16 : k * 32 + 32]
        for h in range(16):
            out[k : k + 1, h * 256 : h * 256 + 256] = both[h : h + 1]


def down(order, parts, g, w, basis, lt):
    return pl.pallas_call(
        down_kernel,
        out_shape=jax.ShapeDtypeStruct((4, 4096), F32),
        in_specs=[HBM] + [VM] * 10 + [HBM] * 2,
        out_specs=VM,
        scratch_shapes=[
            pltpu.VMEM((1, 4096), jnp.int32),
            pltpu.VMEM((16, 256, 256), BF),
            pltpu.VMEM((30, 256, 256), BF),
            pltpu.VMEM((16, 8, 256), F32),
            pltpu.VMEM((16, 256, 256), BF),
            pltpu.SemaphoreType.DMA((9,)),
        ],
        compiler_params=pltpu.CompilerParams(vmem_limit_bytes=16 * MB),
        name="down",
    )(order, *parts, g, w, basis, lt)


def swapped(value, mask):
    return lax.ppermute(value, "leaf", [(i, i ^ mask) for i in range(16)])


def pinned(value):
    return pltpu.with_memory_space_constraint(value, pltpu.HBM)


def tie(*values):
    return lax.optimization_barrier(values)


def shards(points, values, order, block_list, leaf_basis, local_transfers, chain_transfers):
    points, values, order, leaf_basis, local_transfers = map(
        pinned, (points, values, order, leaf_basis, local_transfers)
    )
    shard = chain_transfers.reshape(8, 16, 256)
    pair = shifted(shard, R1[1])
    own, g, root = up(points, values, order, leaf_basis, local_transfers)
    pair, own = tie(pair, own)
    pair = jnp.stack([shard, pair])
    other = shifted(pair, R1[2])
    left = lax.ppermute(own, "leaf", [(i, (i + 1) % 16) for i in range(16)])
    right = lax.ppermute(own, "leaf", [(i, (i - 1) % 16) for i in range(16)])
    base, pt = near_own(own)
    other, base, left, right = tie(other, base, left, right)
    row = jnp.concatenate([pair, other], 0)
    row = jnp.concatenate([row[:, :6], row[:, 7:]], 1)
    groups = [row] + [shifted(row, s) for s in R2[1:]]
    slots = block_list - (lax.axis_index("leaf") * 16 - 16)
    na = near(0, 8, slots, left, own, right, base, pt)
    *groups, na = tie(*groups, na)
    c, w = chain(root, groups)
    o1 = swapped(c, 1)
    s = c[1:] + o1[1:]
    q1 = swapped(s, 2)
    q2 = swapped(s[1:], 4)
    q3 = swapped(s[1:], 6)
    own, _ = tie(own, s)
    nb = near(8, 4, slots, left, own, right, base, pt)
    q1, q2, q3, nb = tie(q1, q2, q3, nb)
    last = s[2:] + q1[2:] + q2[1:] + q3[1:]
    o3 = swapped(last, 12)
    own, _ = tie(own, last)
    nc = near(12, 4, slots, left, own, right, base, pt)
    return down(order, (o1, q1, q2, q3, o3, na, nb, nc), g, w, leaf_basis, local_transfers)


def solution(mesh):
    placed = (
        P(None, "leaf"),
        P("probe", "leaf"),
        P("leaf", None),
        P("leaf", None),
        P("leaf", None, None),
        P("leaf", None, None, None, None),
        P("leaf", None, None, "probe", None),
    )
    return jax.shard_map(
        shards, mesh=mesh, in_specs=placed, out_specs=P("probe", "leaf"), check_vma=False
    )
```

```python
import functools
import jax
import jax.numpy as jnp
from jax import lax
from jax.experimental import pallas as pl
from jax.experimental.pallas import tpu as pltpu
from jax.sharding import PartitionSpec as P

F32 = jnp.float32
BF = jnp.bfloat16
MB = 2**20
NT = (((1,), (1,)), ((), ()))
NN = (((1,), (0,)), ((), ()))
VM = pl.BlockSpec(memory_space=pltpu.VMEM)
SM = pl.BlockSpec(memory_space=pltpu.SMEM)
HBM = pl.BlockSpec(memory_space=pltpu.HBM)


def dot(a, b, dims=NN):
    return lax.dot_general(a, b, dims, preferred_element_type=F32)


def split(s):
    hi = s.astype(BF).astype(F32)
    return jnp.concatenate([hi, s - hi], 0).astype(BF)


def dot2(left, mat, dims=NN):
    r = dot(left, mat, dims)
    return r[:8] + r[8:]


LEVELS = ((0, 16), (16, 8), (24, 4), (28, 2))


def starter(sem):
    copies = []

    def start(src, dst):
        copy = pltpu.make_async_copy(src, dst, sem.at[len(copies)])
        copy.start()
        copies.append(copy)

    return copies, start


def up_kernel(points, values, order, basis, lt, td, g, root, pv, vv, ov, xs, xr, bas, ltv, s, sem):
    copies, start = starter(sem)
    start(points, pv)
    start(values, vv)
    start(order, ov)
    for q in range(2):
        start(basis.at[pl.ds(q * 8, 8)], bas.at[pl.ds(q * 8, 8)])
    for q in range(4):
        start(lt.at[0, pl.ds(q * 4, 4)], ltv.at[pl.ds(q * 4, 4)])
    for q in range(2):
        start(lt.at[0, pl.ds(16 + q * 4, 4)], ltv.at[pl.ds(16 + q * 4, 4)])
    start(lt.at[0, pl.ds(24, 6)], ltv.at[pl.ds(24, 6)])
    for copy in copies[:3]:
        copy.wait()
    xs[0:8, :] = pv[...].astype(F32)
    xs[8:16, :] = jnp.zeros((8, xs.shape[1]), F32)
    xs[8:12, :] = vv[...].astype(F32)
    for h in range(16):
        xr[h * 16 : h * 16 + 16, :] = xs[:, h * 256 : h * 256 + 256].astype(BF)
    rows = lax.broadcasted_iota(jnp.int32, (256, 256), 0)
    sub = lax.broadcasted_iota(jnp.int32, (8, 256), 0)
    for t in range(16):
        o = ov[:, t * 256 : t * 256 + 256]
        oh = jnp.where(rows == (o & 255), 1.0, 0.0).astype(BF)
        z = dot(xr[...], oh)
        hi = o >> 8
        low = jnp.zeros((8, 256), F32)
        high = jnp.zeros((8, 256), F32)
        for h in range(16):
            low = jnp.where(hi == h, z[h * 16 : h * 16 + 8], low)
            high = jnp.where(hi == h, z[h * 16 + 8 : h * 16 + 16], high)
        m = jnp.sum(low * low, 0, keepdims=True) * 0.125
        mh = m.astype(BF).astype(F32)
        high = jnp.where(sub == 4, mh, jnp.where(sub == 5, m - mh, jnp.where(sub >= 6, 1.0, high)))
        td[t] = jnp.concatenate([low, high], 0).astype(BF)
    for l in range(16):
        if l % 8 == 0:
            copies[3 + l // 8].wait()
        r = dot(td[l], bas[l])
        s[l] = jnp.where(sub < 4, r[8:], 0.0)
    for start_slot, count in LEVELS:
        for n in range(0, count, 2):
            slot = start_slot + n
            if slot % 4 == 0 and slot < 24:
                copies[5 + slot // 4].wait()
            if slot == 24:
                copies[11].wait()
            l0 = split(s[n])
            l1 = split(s[n + 1])
            g[slot + 1] = dot2(l0, ltv[slot, 1])
            g[slot] = dot2(l1, ltv[slot + 1, 1])
            s[n // 2] = dot2(l0, ltv[slot, 0]) + dot2(l1, ltv[slot + 1, 0])
    root[...] = s[0]


def up(points, values, order, basis, lt):
    return pl.pallas_call(
        up_kernel,
        out_shape=(
            jax.ShapeDtypeStruct((16, 16, 256), BF),
            jax.ShapeDtypeStruct((30, 8, 256), F32),
            jax.ShapeDtypeStruct((8, 256), F32),
        ),
        in_specs=[HBM] * 5,
        out_specs=(VM, VM, VM),
        scratch_shapes=[
            pltpu.VMEM((8, 4096), BF),
            pltpu.VMEM((4, 4096), BF),
            pltpu.VMEM((1, 4096), jnp.int32),
            pltpu.VMEM((16, 4096), F32),
            pltpu.VMEM((256, 256), BF),
            pltpu.VMEM((16, 256, 256), BF),
            pltpu.VMEM((30, 2, 256, 256), BF),
            pltpu.VMEM((16, 8, 256), F32),
            pltpu.SemaphoreType.DMA((12,)),
        ],
        compiler_params=pltpu.CompilerParams(vmem_limit_bytes=16 * MB),
        name="up",
    )(points, values, order, basis, lt)


def sources(ref):
    p = ref[...].astype(F32)
    sub = lax.broadcasted_iota(jnp.int32, (16, 256), 0)
    m = jnp.sum(jnp.where(sub < 8, p * p, 0.0), 0, keepdims=True) * 0.125 + 1.0
    mh = m.astype(BF).astype(F32)
    p = jnp.where(
        sub < 8,
        p * -0.25,
        jnp.where(sub < 12, 0.0, jnp.where(sub < 14, 1.0, jnp.where(sub == 14, mh, m - mh))),
    )
    return p.T.astype(BF)


def block(pt, q):
    f = dot(pt, q)
    return dot(q, pltpu.reciprocal(f * f * f, approx=True).astype(BF), NT)[8:]


def near_own_kernel(own, out, pt):
    for l in range(16):
        pt[l] = sources(own.at[l])
        out[l] = block(pt[l], own[l])


def near_own(own):
    return pl.pallas_call(
        near_own_kernel,
        out_shape=(
            jax.ShapeDtypeStruct((16, 8, 256), F32),
            jax.ShapeDtypeStruct((16, 256, 16), BF),
        ),
        in_specs=[VM],
        out_specs=(VM, VM),
        compiler_params=pltpu.CompilerParams(vmem_limit_bytes=4 * MB),
        name="near_own",
    )(own)


def near_leaves(first, count, slot_ref, left, own, right, base, pt, out, win):
    slots = slot_ref[...]
    win[0:16] = left[...]
    win[16:32] = own[...]
    win[32:48] = right[...]
    for l in range(first, first + count):
        total = base[l]
        for n in range(1, 8):
            total = total + block(pt[l], win[slots[l, n]])
        out[l - first] = total


def near_kernel(first, count, *refs):
    near_leaves(first, count, *refs)


def near_fetch_kernel(
    first, count, slots, left, own, right, base, pt, order, basis, lt, out, ov, bas, ev, ohs, win, sem
):
    copies, start = starter(sem)
    start(order, ov)
    for at in range(0, 30, 6):
        start(lt.at[0, pl.ds(at, 6), 0], ev.at[pl.ds(at, 6)])
    for at in range(0, 16, 4):
        start(basis.at[pl.ds(at, 4)], bas.at[pl.ds(at, 4)])
    copies[0].wait()
    rows = lax.broadcasted_iota(jnp.int32, (256, 256), 0)
    for t in range(16):
        o = ov[:, t * 256 : t * 256 + 256]
        ohs[t] = jnp.where(rows == (o & 255), 1.0, 0.0).astype(BF)
    near_leaves(first, count, slots, left, own, right, base, pt, out, win)
    for copy in copies[1:]:
        copy.wait()


WINDOW = pltpu.VMEM((48, 16, 256), BF)


def near(first, count, parts):
    return pl.pallas_call(
        functools.partial(near_kernel, first, count),
        out_shape=jax.ShapeDtypeStruct((count, 8, 256), F32),
        in_specs=[VM] * 6,
        out_specs=VM,
        scratch_shapes=[WINDOW],
        compiler_params=pltpu.CompilerParams(vmem_limit_bytes=8 * MB),
        name="near",
    )(*parts)


def near_fetch(first, count, parts, order, basis, lt):
    return pl.pallas_call(
        functools.partial(near_fetch_kernel, first, count),
        out_shape=(
            jax.ShapeDtypeStruct((count, 8, 256), F32),
            jax.ShapeDtypeStruct((1, 4096), jnp.int32),
            jax.ShapeDtypeStruct((16, 256, 256), BF),
            jax.ShapeDtypeStruct((30, 256, 256), BF),
            jax.ShapeDtypeStruct((16, 256, 256), BF),
        ),
        in_specs=[VM] * 6 + [HBM] * 3,
        out_specs=(VM,) * 5,
        scratch_shapes=[WINDOW, pltpu.SemaphoreType.DMA((10,))],
        compiler_params=pltpu.CompilerParams(vmem_limit_bytes=14 * MB),
        name="near_fetch",
    )(*parts, order, basis, lt)


R1 = ((0, 0), (2, 0), (1, 2), (3, 2))
R2 = ((0, 0), (0, 1), (0, 3), (1, 0))


def shifted(value, shift):
    pairs = [
        (y * 4 + x, (y + shift[0]) % 4 * 4 + (x + shift[1]) % 4) for y in range(4) for x in range(4)
    ]
    return lax.ppermute(value, "probe", pairs)


def chain_kernel(*refs):
    root, groups, c, w = refs[0], refs[1:5], refs[5], refs[6]
    me = lax.axis_index("probe")
    y, x = me // 4, lax.rem(me, 4)
    for ky in range(4):
        for kx in range(4):
            sy = lax.rem(y + 8 - R2[ky][0] - R1[kx][0], 4)
            sx = lax.rem(x + 8 - R2[ky][1] - R1[kx][1], 4)
            at = pl.ds(pl.multiple_of((sy * 4 + sx) * 16, 16), 16)
            for m in range(7):
                w[m, at, :] = groups[ky][kx, m]
    u = root[...]
    for k in range(4):
        left = split(u)
        c[k] = dot2(left, w[2 * k + 1 if k < 3 else 6])
        if k < 3:
            u = dot2(left, w[2 * k])


def chain(root, groups):
    return pl.pallas_call(
        chain_kernel,
        out_shape=(jax.ShapeDtypeStruct((4, 8, 256), F32), jax.ShapeDtypeStruct((7, 256, 256), BF)),
        in_specs=[VM] * 5,
        out_specs=(VM, VM),
        compiler_params=pltpu.CompilerParams(vmem_limit_bytes=8 * MB),
        name="chain",
    )(root, *groups)


def down_kernel(o1, q1, q2, q3, o3, na, nb, nc, g, chain, ov, bas, ev, ohs, out, f):
    top = o3[0]
    for term, k in ((q2[0] + q3[0], 2), (q1[0], 1), (o1[0], 0)):
        top = term + dot2(split(top), chain[2 * k], NT)
    f[0] = top
    for start_slot, count in LEVELS[::-1]:
        for m in range(count // 2 - 1, -1, -1):
            slot = start_slot + 2 * m
            l = split(f[m])
            f[2 * m + 1] = g[slot + 1] + dot2(l, ev[slot + 1], NT)
            f[2 * m] = g[slot] + dot2(l, ev[slot], NT)
    near_f = [r[i] for r in (na, nb, nc) for i in range(r.shape[0])]
    hrow = lax.broadcasted_iota(jnp.int32, (16, 256), 0)
    acc = jnp.zeros((128, 256), F32)
    for t in range(16):
        c = near_f[t] + dot2(split(f[t]), bas[t], NT)
        hit = hrow == (ov[:, t * 256 : t * 256 + 256] >> 8)
        ch = c.astype(BF).astype(F32)
        cl = c - ch
        parts = [jnp.where(hit, part[k : k + 1], 0.0) for k in range(4) for part in (ch, cl)]
        acc = acc + dot(jnp.concatenate(parts, 0).astype(BF), ohs[t], NT)
    for k in range(4):
        both = acc[k * 32 : k * 32 + 16] + acc[k * 32 + 16 : k * 32 + 32]
        for h in range(16):
            out[k : k + 1, h * 256 : h * 256 + 256] = both[h : h + 1]


def down(parts, g, w, fetched):
    return pl.pallas_call(
        down_kernel,
        out_shape=jax.ShapeDtypeStruct((4, 4096), F32),
        in_specs=[VM] * 14,
        out_specs=VM,
        scratch_shapes=[pltpu.VMEM((16, 8, 256), F32)],
        compiler_params=pltpu.CompilerParams(vmem_limit_bytes=14 * MB),
        name="down",
    )(*parts, g, w, *fetched)


def swapped(value, mask):
    return lax.ppermute(value, "leaf", [(i, i ^ mask) for i in range(16)])


def pinned(value):
    return pltpu.with_memory_space_constraint(value, pltpu.HBM)


def tie(*values):
    return lax.optimization_barrier(values)


def shards(points, values, order, block_list, leaf_basis, local_transfers, chain_transfers):
    points, values, order, leaf_basis, local_transfers = map(
        pinned, (points, values, order, leaf_basis, local_transfers)
    )
    shard = chain_transfers.reshape(8, 16, 256)
    pair = shifted(shard, R1[1])
    own, g, root = up(points, values, order, leaf_basis, local_transfers)
    pair, own = tie(pair, own)
    pair = jnp.stack([shard, pair])
    other = shifted(pair, R1[2])
    left = lax.ppermute(own, "leaf", [(i, (i + 1) % 16) for i in range(16)])
    right = lax.ppermute(own, "leaf", [(i, (i - 1) % 16) for i in range(16)])
    base, pt = near_own(own)
    other, base, left, right = tie(other, base, left, right)
    row = jnp.concatenate([pair, other], 0)
    row = jnp.concatenate([row[:, :6], row[:, 7:]], 1)
    groups = [row] + [shifted(row, s) for s in R2[1:]]
    slots = block_list - (lax.axis_index("leaf") * 16 - 16)
    parts = (slots, left, own, right, base, pt)
    na = near(0, 9, parts)
    *groups, na = tie(*groups, na)
    c, w = chain(root, groups)
    o1 = swapped(c, 1)
    s = c[1:] + o1[1:]
    q1 = swapped(s, 2)
    q2 = swapped(s[1:], 4)
    q3 = swapped(s[1:], 6)
    own, _ = tie(own, s)
    parts = (slots, left, own, right, base, pt)
    nb = near(9, 4, parts)
    q1, q2, q3, nb = tie(q1, q2, q3, nb)
    last = s[2:] + q1[2:] + q2[1:] + q3[1:]
    o3 = swapped(last, 12)
    own, _ = tie(own, last)
    parts = (slots, left, own, right, base, pt)
    nc, *fetched = near_fetch(13, 3, parts, order, leaf_basis, local_transfers)
    return down((o1, q1, q2, q3, o3, na, nb, nc), g, w, fetched)


def solution(mesh):
    placed = (
        P(None, "leaf"),
        P("probe", "leaf"),
        P("leaf", None),
        P("leaf", None),
        P("leaf", None, None),
        P("leaf", None, None, None, None),
        P("leaf", None, None, "probe", None),
    )
    return jax.shard_map(
        shards, mesh=mesh, in_specs=placed, out_specs=P("probe", "leaf"), check_vma=False
    )
```

```python
import functools
import jax
import jax.numpy as jnp
from jax import lax
from jax.experimental import pallas as pl
from jax.experimental.pallas import tpu as pltpu
from jax.sharding import PartitionSpec as P

F32 = jnp.float32
BF = jnp.bfloat16
MB = 2**20
NT = (((1,), (1,)), ((), ()))
NN = (((1,), (0,)), ((), ()))
VM = pl.BlockSpec(memory_space=pltpu.VMEM)
SM = pl.BlockSpec(memory_space=pltpu.SMEM)
HBM = pl.BlockSpec(memory_space=pltpu.HBM)


def dot(a, b, dims=NN):
    return lax.dot_general(a, b, dims, preferred_element_type=F32)


def split(s):
    hi = s.astype(BF).astype(F32)
    return jnp.concatenate([hi, s - hi], 0).astype(BF)


def dot2(left, mat, dims=NN):
    r = dot(left, mat, dims)
    return r[:8] + r[8:]


LEVELS = ((0, 16), (16, 8), (24, 4), (28, 2))


def starter(sem):
    copies = []

    def start(src, dst):
        copy = pltpu.make_async_copy(src, dst, sem.at[len(copies)])
        copy.start()
        copies.append(copy)

    return copies, start


def up_kernel(points, values, order, basis, lt, td, s0, g, root, pv, vv, ov, xs, xr, bas, ltv, s, sem):
    copies, start = starter(sem)
    start(points, pv)
    start(values, vv)
    start(order, ov)
    for q in range(2):
        start(basis.at[pl.ds(q * 8, 8)], bas.at[pl.ds(q * 8, 8)])
    for q in range(4):
        start(lt.at[0, pl.ds(q * 4, 4), 0], ltv.at[pl.ds(q * 4, 4), 0])
    for q in range(2):
        start(lt.at[0, pl.ds(16 + q * 4, 4)], ltv.at[pl.ds(16 + q * 4, 4)])
    start(lt.at[0, pl.ds(24, 6)], ltv.at[pl.ds(24, 6)])
    for copy in copies[:3]:
        copy.wait()
    xs[0:8, :] = pv[...].astype(F32)
    xs[8:16, :] = jnp.zeros((8, xs.shape[1]), F32)
    xs[8:12, :] = vv[...].astype(F32)
    for h in range(16):
        xr[h * 16 : h * 16 + 16, :] = xs[:, h * 256 : h * 256 + 256].astype(BF)
    rows = lax.broadcasted_iota(jnp.int32, (256, 256), 0)
    sub = lax.broadcasted_iota(jnp.int32, (8, 256), 0)
    for t in range(16):
        o = ov[:, t * 256 : t * 256 + 256]
        oh = jnp.where(rows == (o & 255), 1.0, 0.0).astype(BF)
        z = dot(xr[...], oh)
        hi = o >> 8
        low = jnp.zeros((8, 256), F32)
        high = jnp.zeros((8, 256), F32)
        for h in range(16):
            low = jnp.where(hi == h, z[h * 16 : h * 16 + 8], low)
            high = jnp.where(hi == h, z[h * 16 + 8 : h * 16 + 16], high)
        m = jnp.sum(low * low, 0, keepdims=True) * 0.125
        mh = m.astype(BF).astype(F32)
        high = jnp.where(sub == 4, mh, jnp.where(sub == 5, m - mh, jnp.where(sub >= 6, 1.0, high)))
        td[t] = jnp.concatenate([low, high], 0).astype(BF)
    for l in range(16):
        if l % 8 == 0:
            copies[3 + l // 8].wait()
        r = dot(td[l], bas[l])
        s0[l] = jnp.where(sub < 4, r[8:], 0.0)
    for start_slot, count in LEVELS:
        for n in range(0, count, 2):
            slot = start_slot + n
            if slot % 4 == 0 and slot < 24:
                copies[5 + slot // 4].wait()
            if slot == 24:
                copies[11].wait()
            level = s if start_slot else s0
            l0 = split(level[n])
            l1 = split(level[n + 1])
            if start_slot:
                g[slot - 15] = dot2(l0, ltv[slot, 1])
                g[slot - 16] = dot2(l1, ltv[slot + 1, 1])
            s[n // 2] = dot2(l0, ltv[slot, 0]) + dot2(l1, ltv[slot + 1, 0])
    root[...] = s[0]


def up(points, values, order, basis, lt):
    return pl.pallas_call(
        up_kernel,
        out_shape=(
            jax.ShapeDtypeStruct((16, 16, 256), BF),
            jax.ShapeDtypeStruct((16, 8, 256), F32),
            jax.ShapeDtypeStruct((14, 8, 256), F32),
            jax.ShapeDtypeStruct((8, 256), F32),
        ),
        in_specs=[HBM] * 5,
        out_specs=(VM,) * 4,
        scratch_shapes=[
            pltpu.VMEM((8, 4096), BF),
            pltpu.VMEM((4, 4096), BF),
            pltpu.VMEM((1, 4096), jnp.int32),
            pltpu.VMEM((16, 4096), F32),
            pltpu.VMEM((256, 256), BF),
            pltpu.VMEM((16, 256, 256), BF),
            pltpu.VMEM((30, 2, 256, 256), BF),
            pltpu.VMEM((16, 8, 256), F32),
            pltpu.SemaphoreType.DMA((12,)),
        ],
        compiler_params=pltpu.CompilerParams(vmem_limit_bytes=16 * MB),
        name="up",
    )(points, values, order, basis, lt)


def sources(ref):
    p = ref[...].astype(F32)
    sub = lax.broadcasted_iota(jnp.int32, (16, 256), 0)
    m = jnp.sum(jnp.where(sub < 8, p * p, 0.0), 0, keepdims=True) * 0.125 + 1.0
    mh = m.astype(BF).astype(F32)
    p = jnp.where(
        sub < 8,
        p * -0.25,
        jnp.where(sub < 12, 0.0, jnp.where(sub < 14, 1.0, jnp.where(sub == 14, mh, m - mh))),
    )
    return p.T.astype(BF)


def block(pt, q):
    f = dot(pt, q)
    return dot(q, pltpu.reciprocal(f * f * f, approx=True).astype(BF), NT)[8:]


def near_own_kernel(own, s0, lt, out, pt, g, cv, sem):
    copies, start = starter(sem)
    for q in range(2):
        start(lt.at[0, pl.ds(q * 8, 8), 1], cv.at[pl.ds(q * 8, 8)])
    for l in range(16):
        pt[l] = sources(own.at[l])
        out[l] = block(pt[l], own[l])
    for l in range(16):
        if l % 8 == 0:
            copies[l // 8].wait()
        g[l ^ 1] = dot2(split(s0[l]), cv[l])


def near_own(own, s0, lt):
    return pl.pallas_call(
        near_own_kernel,
        out_shape=(
            jax.ShapeDtypeStruct((16, 8, 256), F32),
            jax.ShapeDtypeStruct((16, 256, 16), BF),
            jax.ShapeDtypeStruct((16, 8, 256), F32),
        ),
        in_specs=[VM, VM, HBM],
        out_specs=(VM,) * 3,
        scratch_shapes=[pltpu.VMEM((16, 256, 256), BF), pltpu.SemaphoreType.DMA((2,))],
        compiler_params=pltpu.CompilerParams(vmem_limit_bytes=6 * MB),
        name="near_own",
    )(own, s0, lt)


def near_leaves(first, count, slot_ref, left, own, right, base, pt, out, win):
    slots = slot_ref[...]
    win[0:16] = left[...]
    win[16:32] = own[...]
    win[32:48] = right[...]
    for l in range(first, first + count):
        total = base[l]
        for n in range(1, 8):
            total = total + block(pt[l], win[slots[l, n]])
        out[l - first] = total


def near_kernel(first, count, *refs):
    near_leaves(first, count, *refs)


def near_fetch_kernel(
    first, count, slots, left, own, right, base, pt, order, basis, lt, out, ov, bas, ev, ohs, win, sem
):
    copies, start = starter(sem)
    start(order, ov)
    for at in range(0, 30, 15):
        start(lt.at[0, pl.ds(at, 15), 0], ev.at[pl.ds(at, 15)])
    start(basis, bas)
    copies[0].wait()
    rows = lax.broadcasted_iota(jnp.int32, (256, 256), 0)
    for t in range(16):
        o = ov[:, t * 256 : t * 256 + 256]
        ohs[t] = jnp.where(rows == (o & 255), 1.0, 0.0).astype(BF)
    near_leaves(first, count, slots, left, own, right, base, pt, out, win)
    for copy in copies[1:]:
        copy.wait()


WINDOW = pltpu.VMEM((48, 16, 256), BF)


def near(first, count, parts):
    return pl.pallas_call(
        functools.partial(near_kernel, first, count),
        out_shape=jax.ShapeDtypeStruct((count, 8, 256), F32),
        in_specs=[VM] * 6,
        out_specs=VM,
        scratch_shapes=[WINDOW],
        compiler_params=pltpu.CompilerParams(vmem_limit_bytes=8 * MB),
        name="near",
    )(*parts)


def near_fetch(first, count, parts, order, basis, lt):
    return pl.pallas_call(
        functools.partial(near_fetch_kernel, first, count),
        out_shape=(
            jax.ShapeDtypeStruct((count, 8, 256), F32),
            jax.ShapeDtypeStruct((1, 4096), jnp.int32),
            jax.ShapeDtypeStruct((16, 256, 256), BF),
            jax.ShapeDtypeStruct((30, 256, 256), BF),
            jax.ShapeDtypeStruct((16, 256, 256), BF),
        ),
        in_specs=[VM] * 6 + [HBM] * 3,
        out_specs=(VM,) * 5,
        scratch_shapes=[WINDOW, pltpu.SemaphoreType.DMA((4,))],
        compiler_params=pltpu.CompilerParams(vmem_limit_bytes=14 * MB),
        name="near_fetch",
    )(*parts, order, basis, lt)


R1 = ((0, 0), (2, 0), (1, 2), (3, 2))
R2 = ((0, 0), (0, 1), (0, 3), (1, 0))


def shifted(value, shift):
    pairs = [
        (y * 4 + x, (y + shift[0]) % 4 * 4 + (x + shift[1]) % 4) for y in range(4) for x in range(4)
    ]
    return lax.ppermute(value, "probe", pairs)


def chain_kernel(*refs):
    root, groups, c, w = refs[0], refs[1:5], refs[5], refs[6]
    me = lax.axis_index("probe")
    y, x = me // 4, lax.rem(me, 4)
    for ky in range(4):
        for kx in range(4):
            sy = lax.rem(y + 8 - R2[ky][0] - R1[kx][0], 4)
            sx = lax.rem(x + 8 - R2[ky][1] - R1[kx][1], 4)
            at = pl.ds(pl.multiple_of((sy * 4 + sx) * 16, 16), 16)
            for m in range(7):
                w[m, at, :] = groups[ky][kx, m]
    u = root[...]
    for k in range(4):
        left = split(u)
        c[k] = dot2(left, w[2 * k + 1 if k < 3 else 6])
        if k < 3:
            u = dot2(left, w[2 * k])


def chain(root, groups):
    return pl.pallas_call(
        chain_kernel,
        out_shape=(jax.ShapeDtypeStruct((4, 8, 256), F32), jax.ShapeDtypeStruct((7, 256, 256), BF)),
        in_specs=[VM] * 5,
        out_specs=(VM, VM),
        compiler_params=pltpu.CompilerParams(vmem_limit_bytes=8 * MB),
        name="chain",
    )(root, *groups)


def down_kernel(o1, q1, q2, q3, o3, na, nb, nc, g0, g1, chain, ov, bas, ev, ohs, out, f):
    g = [g0[i] for i in range(16)] + [g1[i] for i in range(14)]
    top = o3[0]
    for term, k in ((q2[0] + q3[0], 2), (q1[0], 1), (o1[0], 0)):
        top = term + dot2(split(top), chain[2 * k], NT)
    f[0] = top
    for start_slot, count in LEVELS[::-1]:
        for m in range(count // 2 - 1, -1, -1):
            slot = start_slot + 2 * m
            l = split(f[m])
            f[2 * m + 1] = g[slot + 1] + dot2(l, ev[slot + 1], NT)
            f[2 * m] = g[slot] + dot2(l, ev[slot], NT)
    near_f = [r[i] for r in (na, nb, nc) for i in range(r.shape[0])]
    hrow = lax.broadcasted_iota(jnp.int32, (16, 256), 0)
    acc = jnp.zeros((128, 256), F32)
    for t in range(16):
        c = near_f[t] + dot2(split(f[t]), bas[t], NT)
        hit = hrow == (ov[:, t * 256 : t * 256 + 256] >> 8)
        ch = c.astype(BF).astype(F32)
        cl = c - ch
        parts = [jnp.where(hit, part[k : k + 1], 0.0) for k in range(4) for part in (ch, cl)]
        acc = acc + dot(jnp.concatenate(parts, 0).astype(BF), ohs[t], NT)
    for k in range(4):
        both = acc[k * 32 : k * 32 + 16] + acc[k * 32 + 16 : k * 32 + 32]
        for h in range(16):
            out[k : k + 1, h * 256 : h * 256 + 256] = both[h : h + 1]


def down(parts, g0, g1, w, fetched):
    return pl.pallas_call(
        down_kernel,
        out_shape=jax.ShapeDtypeStruct((4, 4096), F32),
        in_specs=[VM] * 15,
        out_specs=VM,
        scratch_shapes=[pltpu.VMEM((16, 8, 256), F32)],
        compiler_params=pltpu.CompilerParams(vmem_limit_bytes=14 * MB),
        name="down",
    )(*parts, g0, g1, w, *fetched)


def swapped(value, mask):
    return lax.ppermute(value, "leaf", [(i, i ^ mask) for i in range(16)])


def pinned(value):
    return pltpu.with_memory_space_constraint(value, pltpu.HBM)


def tie(*values):
    return lax.optimization_barrier(values)


def shards(points, values, order, block_list, leaf_basis, local_transfers, chain_transfers):
    points, values, order, leaf_basis, local_transfers = map(
        pinned, (points, values, order, leaf_basis, local_transfers)
    )
    shard = chain_transfers.reshape(8, 16, 256)
    pair = shifted(shard, R1[1])
    own, s0, g, root = up(points, values, order, leaf_basis, local_transfers)
    pair, own = tie(pair, own)
    pair = jnp.stack([shard, pair])
    other = shifted(pair, R1[2])
    left = lax.ppermute(own, "leaf", [(i, (i + 1) % 16) for i in range(16)])
    right = lax.ppermute(own, "leaf", [(i, (i - 1) % 16) for i in range(16)])
    base, pt, g0 = near_own(own, s0, local_transfers)
    other, base, left, right = tie(other, base, left, right)
    row = jnp.concatenate([pair, other], 0)
    row = jnp.concatenate([row[:, :6], row[:, 7:]], 1)
    groups = [row] + [shifted(row, s) for s in R2[1:]]
    slots = block_list - (lax.axis_index("leaf") * 16 - 16)
    parts = (slots, left, own, right, base, pt)
    na = near(0, 9, parts)
    *groups, na = tie(*groups, na)
    c, w = chain(root, groups)
    o1 = swapped(c, 1)
    s = c[1:] + o1[1:]
    q1 = swapped(s, 2)
    q2 = swapped(s[1:], 4)
    q3 = swapped(s[1:], 6)
    own, _ = tie(own, s)
    parts = (slots, left, own, right, base, pt)
    nb = near(9, 4, parts)
    q1, q2, q3, nb = tie(q1, q2, q3, nb)
    last = s[2:] + q1[2:] + q2[1:] + q3[1:]
    o3 = swapped(last, 12)
    own, _ = tie(own, last)
    parts = (slots, left, own, right, base, pt)
    nc, *fetched = near_fetch(13, 3, parts, order, leaf_basis, local_transfers)
    return down((o1, q1, q2, q3, o3, na, nb, nc), g0, g, w, fetched)


def solution(mesh):
    placed = (
        P(None, "leaf"),
        P("probe", "leaf"),
        P("leaf", None),
        P("leaf", None),
        P("leaf", None, None),
        P("leaf", None, None, None, None),
        P("leaf", None, None, "probe", None),
    )
    return jax.shard_map(
        shards, mesh=mesh, in_specs=placed, out_specs=P("probe", "leaf"), check_vma=False
    )
```
